256 devices in a mesh: hst: 32 (over x_lo, z, core), tp: 8 (over y, x_hi).
Axes of the slice: x: 4 (x_hi: 2, x_lo: 2; x = x_hi * 2 + x_lo), y: 4, z: 8, core: 2. Of those that a mesh axis runs over, the one named last changes fastest.
Arguments:
- queries: bfloat16 [16384, 4096], P('hst', 'tp'), may hold values from -94 to 94
- key_states: bfloat16 [16384, 1024], P('hst', 'tp'), may hold values from -8.5 to 8.5
- value_states: bfloat16 [16384, 1024], P('hst', 'tp'), may hold values from -15 to 15
- passing: int32 [32, 256], P('hst'), may hold values from 0 to 511, as said below
- out_weight: bfloat16 [4096, 7168], P('tp'), may hold values from -0.5 to 0.5
- residual: bfloat16 [16384, 7168], P(('hst', 'tp')), may hold values from -6 to 6
- norm_gain: bfloat16 [7168], replicated, may hold values from 0.5 to 1.5
Outputs:
- stream: bfloat16 [16384, 7168], P(('hst', 'tp'))
- normed: bfloat16 [16384, 7168], P(('hst', 'tp'))
The draws below stay inside these ranges and needn't reach their ends.
Inputs may be any that keep to these rules, and one draw needn't show every extreme that they name: `passing`: each row lists 256 different positions within its block; the first is 0 and the last is 511.
All inputs are finite; a program needn't handle non-finite values.
Results may differ from the reference program's by a relative error of at most 0.018.
Values may be sent and summed in bfloat16 or wider, within the bound.
A program may use at most 192 MiB of HBM per device.

```python
import math
import jax
import jax.numpy as jnp
from jax import lax

D = 7168
KVH = 8
HEAD = 128
GROUP = 4
BLK = 512
QH = 32
RET = 256
BLOCKS = 32
TOKENS = 16384
N_TP = 8


def base_keys(key):
    return jnp.clip(1.4 * jax.random.normal(key, (TOKENS, KVH * HEAD), jnp.float32), -8.4, 8.4)


def draw_key_states(key, part):
    raw = base_keys(key)
    return raw.astype(jnp.bfloat16)


def draw_queries(key, part):
    key = jax.random.fold_in(key, 5)
    raw = jnp.clip(1.4 * jax.random.normal(key, (TOKENS, QH * HEAD), jnp.float32), -8.4, 8.4)
    return raw.astype(jnp.bfloat16)


def draw_passing(key, part):
    key = jax.random.fold_in(key, 9)
    subkeys = jax.random.split(key, BLOCKS)

    def one_row(subkey):
        middle = jax.random.permutation(subkey, BLK - 2)[:RET - 2] + 1
        return jnp.concatenate([jnp.zeros((1,), jnp.int32), middle.astype(jnp.int32), jnp.full((1,), BLK - 1, jnp.int32)])
    return jax.vmap(one_row)(subkeys)


def block_levels(key, extent, cuts, low, top_value):
    factor_of = 1.0
    for position, parts in cuts:
        steps = jax.random.uniform(jax.random.fold_in(jax.random.fold_in(key, 6), position), (parts,), jnp.float32, low / len(cuts), top_value / len(cuts))
        factor_of = factor_of * jnp.repeat(jnp.exp(steps), extent[position] // parts).reshape((-1,) + (1,) * (len(extent) - 1 - position))
    return factor_of


def scatter_about(key, extent, scale, bound, shards=(), kind=jnp.bfloat16):
    array = scale * jax.random.normal(key, extent, jnp.float32)
    if shards:
        array = array * block_levels(key, extent, shards, -0.22, 0.18)
    return jnp.clip(array, -bound, bound).astype(kind)


def setup_inputs(seed: int = 0) -> dict:
    key_of = jax.random.split(jax.random.key(seed), 8)
    return {
        "queries": draw_queries(jax.random.fold_in(key_of[7], 71), 0),
        "key_states": draw_key_states(jax.random.fold_in(key_of[7], 71), 0),
        "value_states": scatter_about(key_of[2], (TOKENS, KVH * HEAD), 3.0, 15.0, ((0, 32), (1, 8))),
        "passing": draw_passing(jax.random.fold_in(key_of[7], 71), 0),
        "out_weight": scatter_about(key_of[4], (QH * HEAD, D), HEAD ** -0.5, 0.5, ((0, 8),)),
        "residual": scatter_about(key_of[5], (TOKENS, D), 1.0, 6.0, ((0, 256),)),
        "norm_gain": jnp.clip(1.0 + 0.1 * jax.random.normal(key_of[6], (D,), jnp.float32), 0.5, 1.5).astype(jnp.bfloat16),
    }


def attend_block(block_index, queries, key_states, value_states, passing):
    first_row = (block_index * BLK).astype(jnp.int32)
    query_rows = lax.dynamic_slice_in_dim(queries, first_row, BLK, 0).reshape(BLK, QH, HEAD)
    own_keys = lax.dynamic_slice_in_dim(key_states, first_row, BLK, 0)
    own_values = lax.dynamic_slice_in_dim(value_states, first_row, BLK, 0)
    offsets = (jnp.arange(BLOCKS, dtype=jnp.int32) * BLK)[:, None]
    flat_rows = (passing.astype(jnp.int32) + offsets).reshape(BLOCKS * RET)
    kept_keys = key_states[flat_rows]
    kept_values = value_states[flat_rows]
    all_keys = jnp.concatenate([own_keys, key_states[:BLK], kept_keys], axis=0)
    all_values = jnp.concatenate([own_values, value_states[:BLK], kept_values], axis=0)
    positions = jnp.arange(BLK, dtype=jnp.int32)
    causal = positions[None, :] <= positions[:, None]
    anchor_seen = jnp.broadcast_to(block_index >= 1, (BLK, BLK))
    root = jnp.arange(BLOCKS * RET, dtype=jnp.int32) // RET
    kept_seen = jnp.broadcast_to(((root >= 1) & (root <= block_index - 1))[None, :], (BLK, BLOCKS * RET))
    visible = jnp.concatenate([causal, anchor_seen, kept_seen], axis=1)

    def one_head(key_head):
        chosen = lax.dynamic_slice_in_dim(query_rows, (key_head * GROUP).astype(jnp.int32), GROUP, 1).astype(jnp.float32)
        head_keys = lax.dynamic_slice_in_dim(all_keys, (key_head * HEAD).astype(jnp.int32), HEAD, 1).astype(jnp.float32)
        head_values = lax.dynamic_slice_in_dim(all_values, (key_head * HEAD).astype(jnp.int32), HEAD, 1).astype(jnp.float32)
        scores = jnp.einsum('igd,jd->gij', chosen, head_keys) / math.sqrt(HEAD)
        scores = jnp.where(visible[None], scores, -jnp.inf)
        peak = lax.optimization_barrier(jnp.max(scores, axis=2, keepdims=True))
        expd = jnp.exp(scores - peak)
        total = lax.optimization_barrier(jnp.sum(expd, axis=2, keepdims=True))
        weights = lax.optimization_barrier(expd.astype(jnp.bfloat16)).astype(jnp.float32)
        result = jnp.einsum('gij,jd->gid', weights, head_values) / total
        return result.astype(jnp.bfloat16)
    heads_out = lax.map(one_head, jnp.arange(KVH, dtype=jnp.int32))
    return jnp.transpose(heads_out, (2, 0, 1, 3)).reshape(BLK, QH * HEAD)

def reference(queries, key_states, value_states, passing, out_weight, residual, norm_gain):
    blocks_out = lax.map(lambda index_value: attend_block(index_value, queries, key_states, value_states, passing), jnp.arange(BLOCKS, dtype=jnp.int32))
    attended = blocks_out.reshape(TOKENS, QH * HEAD)
    group_cols = QH * HEAD // N_TP
    combined = residual.astype(jnp.float32)
    for tp_group in range(N_TP):
        partial_value = jnp.dot(attended[:, tp_group * group_cols:(tp_group + 1) * group_cols], out_weight[tp_group * group_cols:(tp_group + 1) * group_cols], preferred_element_type=jnp.float32)
        combined = combined + lax.optimization_barrier(partial_value.astype(jnp.bfloat16)).astype(jnp.float32)
    stream = combined.astype(jnp.bfloat16)
    spread = lax.optimization_barrier(jnp.mean(combined * combined, axis=1, keepdims=True))
    normed = (combined * lax.rsqrt(spread + 1e-05) * norm_gain.astype(jnp.float32)).astype(jnp.bfloat16)
    return (stream, normed)
```

```python
import math

import jax
import jax.numpy as jnp
from jax import lax
from jax.experimental import pallas as pl
from jax.experimental.pallas import tpu as pltpu
from jax.sharding import PartitionSpec as P

f32 = jnp.float32
bf16 = jnp.bfloat16
MESH = pl.DeviceIdType.MESH

HEAD = 128
HEADS = 4
BLK = 512
RET = 256
D = 7168
HALF = D // 2
CC = 512
NCH = HALF // CC
QT = 128
LAST = 31
SCALE = math.log2(math.e) / math.sqrt(HEAD)
ROWS = 256
TILES = HEADS * BLK // ROWS
GKEYS = 4 * RET


def kernel(
    q_ref,
    k_ref,
    v_ref,
    pass_ref,
    w_ref,
    res_ref,
    gain_ref,
    stream_ref,
    normed_ref,
    kvbuf,
    qs,
    acc,
    peak,
    wall,
    abuf,
    ast,
    p0buf,
    prec,
    p1buf,
    xsend,
    xrec,
    ssend,
    srec,
    comb,
    resbuf,
    an_send,
    an_recv,
    x_send,
    x_recv,
    z_send,
    z_recv,
    s_send,
    s_recv,
    wl_sem,
    w_send,
    w_recv,
    a_send,
    a_recv,
    y_send,
    y_recv,
    xh_send,
    xh_recv,
    sb_send,
    sb_recv,
    res_sem,
):
    h = lax.axis_index("hst")
    t = lax.axis_index("tp")
    x = h // 16
    z = (h // 2) % 8
    c = h % 2
    y = t // 2
    e = t % 2
    turn = 1 - 2 * (y % 2)
    pr = (y + turn + 2 * c + 4) % 4
    nb = (y + turn + 2 * (1 - c) + 4) % 4

    def dev(x_, z_, c_, y_, e_):
        return (x_ * 16 + z_ * 2 + c_, y_ * 2 + e_)

    x_dev = dev(1 - x, z, c, y, e)
    up_dev = dev(x, (z + 1) % 8, c, y, e)
    down_dev = dev(x, (z + 7) % 8, c, y, e)
    sib_dev = dev(x, z, 1 - c, y, e)
    pr_dev = dev(x, z, c, pr, e)
    pr_cross = dev(x, z, 1 - c, pr, e)
    nb_dev = dev(x, z, c, nb, e)
    nb_cross = dev(x, z, 1 - c, nb, e)
    e_dev = dev(x, z, c, y, 1 - e)
    e_cross = dev(x, z, 1 - c, y, 1 - e)
    partners = (
        x_dev,
        up_dev,
        down_dev,
        sib_dev,
        pr_dev,
        pr_cross,
        nb_dev,
        nb_cross,
        e_dev,
        e_cross,
    )

    def remote(src, dst, send, recv, device):
        return pltpu.make_async_remote_copy(
            src_ref=src,
            dst_ref=dst,
            send_sem=send,
            recv_sem=recv,
            device_id=device,
            device_id_type=MESH,
        )

    col0 = c * HALF

    def w_cols(j):
        return pl.ds(pl.multiple_of(col0 + j * CC, 128), CC)

    def w_local(j):
        return pltpu.make_async_copy(
            w_ref.at[:, w_cols(j)], wall.at[j, pl.ds(0, BLK), :], wl_sem.at[j]
        )

    def w_remote(j):
        return remote(
            w_ref.at[:, w_cols(j)],
            wall.at[j, pl.ds(BLK, BLK), :],
            w_send.at[j],
            w_recv.at[j],
            pr_dev,
        )

    res_copy = pltpu.make_async_copy(res_ref, resbuf, res_sem)

    barrier = pltpu.get_barrier_semaphore()
    for partner in partners:
        pl.semaphore_signal(barrier, inc=1, device_id=partner, device_id_type=MESH)

    @pl.when(h == 0)
    def _():
        pl.semaphore_signal(barrier, inc=1, device_id=(LAST, t), device_id_type=MESH)

    @pl.when(h == LAST)
    def _():
        pl.semaphore_signal(barrier, inc=1, device_id=(0, t), device_id_type=MESH)

    lane = lax.broadcasted_iota(jnp.int32, (BLK, RET), 1)
    sub = lax.broadcasted_iota(jnp.int32, (BLK, RET), 0)
    chosen = jnp.where(h == 0, lane, jnp.broadcast_to(pass_ref[...], (BLK, RET)))
    onehot = (sub == chosen).astype(bf16)
    both = jnp.concatenate([k_ref[...], v_ref[...]], axis=1)
    kept = lax.dot_general(
        onehot, both, (((0,), (0,)), ((), ())), preferred_element_type=f32
    ).astype(bf16)

    @pl.when(h != LAST)
    def _():
        kvbuf[z, c, x, 0] = kept[:, :HEAD]
        kvbuf[z, c, x, 1] = kept[:, HEAD:]

    extra = jnp.where((h == 0) | (h == LAST), 1, 0)
    pl.semaphore_wait(barrier, len(partners) + extra)

    def anchor(i):
        src = (k_ref, v_ref)[i].at[pl.ds(RET, RET), :]
        return remote(src, kvbuf.at[7, 1, 1, i], an_send.at[i], an_recv.at[i], (LAST, t))

    def anchor_in(i):
        src = (k_ref, v_ref)[i].at[pl.ds(RET, RET), :]
        return remote(src, kvbuf.at[7, 1, 1, i], an_send.at[i], an_recv.at[i], (0, t))

    @pl.when(h == 0)
    def _():
        anchor(0).start()
        anchor(1).start()

    @pl.when(h == LAST)
    def _():
        anchor_in(0).wait_recv()
        anchor_in(1).wait_recv()

    def slot(z_, x_):
        return kvbuf.at[z_, c, x_]

    def x_copy():
        return remote(slot(z, x), slot(z, x), x_send.at[0], x_recv.at[0], x_dev)

    def z_copy(direction, d, z_, x_):
        device = up_dev if direction == 0 else down_dev
        return remote(
            slot(z_, x_),
            slot(z_, x_),
            z_send.at[direction, d, x_],
            z_recv.at[direction, d, x_],
            device,
        )

    def s_copy(g, z_, x_):
        return remote(slot(z_, x_), slot(z_, x_), s_send.at[g, x_], s_recv.at[g, x_], sib_dev)

    def s_wait(g, z_, x_):
        theirs = kvbuf.at[z_, 1 - c, x_]
        remote(theirs, theirs, s_send.at[g, x_], s_recv.at[g, x_], sib_dev).wait_recv()

    x_copy().start()
    z_copy(0, 0, z, x).start()
    z_copy(1, 0, z, x).start()
    s_copy(0, z, x).start()
    for j in range(NCH):
        w_remote(j).start()
    for j in range(NCH):
        w_local(j).start()
    res_copy.start()

    quarters = ((y + 2) % 4, pr, nb, y)
    for r in range(4):
        rows = pl.ds(pl.multiple_of(quarters[r] * QT, QT), QT)
        for head in range(HEADS):
            scaled = q_ref[rows, head * HEAD : (head + 1) * HEAD].astype(f32) * SCALE
            high = scaled.astype(bf16)
            low = (scaled - high.astype(f32)).astype(bf16)
            qs[r, head * QT : (head + 1) * QT, :HEAD] = high
            qs[r, head * QT : (head + 1) * QT, HEAD:] = low

    def logits(tile, keys2):
        r, half = tile // 2, tile % 2
        return lax.dot_general(
            qs[r, half * ROWS : (half + 1) * ROWS, :],
            keys2,
            (((1,), (1,)), ((), ())),
            preferred_element_type=f32,
        )

    own_keys = jnp.concatenate([k_ref[...], k_ref[...]], axis=1)
    own_values = jnp.concatenate([v_ref[...], jnp.ones((BLK, HEAD), bf16)], axis=1)
    key_at = lax.broadcasted_iota(jnp.int32, (ROWS, BLK), 1)
    row_at = lax.broadcasted_iota(jnp.int32, (ROWS, BLK), 0) % QT
    for tile in range(TILES):
        scores = logits(tile, own_keys)
        seen = key_at <= row_at + quarters[tile // 2] * QT
        scores = jnp.where(seen, scores, -jnp.inf)
        newest = jnp.max(scores, axis=1, keepdims=True)
        weights = jnp.exp2(scores - newest).astype(bf16)
        rows = pl.ds(tile * ROWS, ROWS)
        peak[rows, :] = jnp.broadcast_to(newest, (ROWS, HEAD))
        acc[rows, :] = jnp.dot(weights, own_values, preferred_element_type=f32)

    x_copy().wait_recv()
    z_copy(0, 0, z, 1 - x).start()
    z_copy(1, 0, z, 1 - x).start()
    s_copy(0, z, 1 - x).start()

    first_key = k_ref[0:1, :]

    def pass_on(d):
        for direction in range(2):
            z_ = (z + 8 - d) % 8 if direction == 0 else (z + d) % 8
            g = 2 * d - 1 + direction
            for x_ in range(2):
                z_copy(direction, d - 1, z_, x_).wait_recv()
                if x_ == direction:
                    z_copy(direction, d, z_, x_).start()
                else:

                    @pl.when(d < 3)
                    def _():
                        z_copy(direction, d, z_, x_).start()

                s_copy(g, z_, x_).start()

    def one_group(g, carry):
        step = (g + 1) // 2
        z_ = (z + 8 + step * (1 - 2 * (g % 2))) % 8

        @pl.when((g % 2 == 1) & (g < 7))
        def _():
            pass_on(step)

        @pl.when(g == 7)
        def _():
            for x_ in range(2):
                z_copy(x_, 3, z_, x_).wait_recv()
                s_copy(g, z_, x_).start()

        for x_ in range(2):
            s_wait(g, z_, x_)

        lowest = z_ * 2
        used = (h >= 1) & ((lowest < h) | (z_ == 7))

        @pl.when(used)
        def _():
            key_parts, value_parts, unit_parts = [], [], []
            for c_ in range(2):
                for x_ in range(2):
                    number = x_ * 16 + z_ * 2 + c_
                    shown = (number < h) | (number == LAST)
                    key_parts.append(jnp.where(shown, kvbuf[z_, c_, x_, 0], first_key))
                    value_parts.append(
                        jnp.where(shown, kvbuf[z_, c_, x_, 1], jnp.zeros((RET, HEAD), bf16))
                    )
                    unit_parts.append(
                        jnp.where(shown, jnp.ones((RET, HEAD), bf16), jnp.zeros((RET, HEAD), bf16))
                    )
            keys = jnp.concatenate(key_parts, axis=0)
            keys2 = jnp.concatenate([keys, keys], axis=1)
            values2 = jnp.concatenate(
                [jnp.concatenate(value_parts, axis=0), jnp.concatenate(unit_parts, axis=0)], axis=1
            )
            all_scores = [logits(tile, keys2) for tile in range(TILES)]
            for tile in range(TILES):
                scores = all_scores[tile]
                rows = pl.ds(tile * ROWS, ROWS)
                before = peak[rows, :]
                newest = jnp.maximum(before, jnp.max(scores, axis=1, keepdims=True))
                shrink = jnp.exp2(before - newest)
                peak[rows, :] = newest
                weights = jnp.exp2(scores - newest[:, :1]).astype(bf16)
                added = jnp.dot(weights, values2, preferred_element_type=f32)
                old = acc[rows, :]
                acc[rows, :] = (
                    jnp.concatenate([old[:, :HEAD] * shrink, old[:, HEAD:] * shrink], axis=1) + added
                )

        return carry

    lax.fori_loop(0, 8, one_group, 0)

    def attended(r, put):
        for head in range(HEADS):
            rows = pl.ds(r * HEADS * QT + head * QT, QT)
            value = (acc[rows, :HEAD] / acc[rows, HEAD:]).astype(bf16)
            put(head, value)

    def put_ast(r):
        def put(head, value):
            ast[r, :, head * HEAD : (head + 1) * HEAD] = value

        return put

    def put_own(tok):
        def put(head, value):
            abuf[tok, 0, c, :, head * HEAD : (head + 1) * HEAD] = value

        return put

    def a_copy(n, src, tok, source, device):
        return remote(
            src, abuf.at[tok, source, c], a_send.at[n], a_recv.at[tok, source, c], device
        )

    def a_copies():
        return (
            a_copy(0, ast.at[0], 0, 1, pr_dev),
            a_copy(1, ast.at[0], 0, 1, nb_cross),
            a_copy(2, ast.at[1], 1, 1, pr_dev),
            a_copy(3, ast.at[1], 0, 0, sib_dev),
            a_copy(4, abuf.at[0, 0, c], 1, 1, nb_cross),
            a_copy(5, abuf.at[1, 0, c], 1, 0, sib_dev),
        )

    copies = a_copies()
    attended(0, put_ast(0))
    copies[0].start()
    copies[1].start()
    attended(1, put_ast(1))
    copies[3].start()
    copies[2].start()
    attended(2, put_own(0))
    copies[4].start()
    attended(3, put_own(1))
    copies[5].start()

    def a_wait(tok, source, block, device):
        ref = abuf.at[tok, source, block]
        remote(ref, ref, a_send.at[0], a_recv.at[tok, source, block], device).wait_recv()

    def project(tok, j):
        total = None
        for source in range(2):
            rows = abuf[tok, source].reshape(2 * QT, BLK)
            term = jnp.dot(
                rows, wall[j, source * BLK : (source + 1) * BLK, :], preferred_element_type=f32
            )
            total = term if total is None else total + term
        return total

    def y_copy(j):
        return remote(p0buf.at[j], prec.at[j], y_send.at[j], y_recv.at[j], nb_dev)

    a_wait(0, 0, 1 - c, sib_dev)
    a_wait(0, 1, c, pr_dev)
    a_wait(0, 1, 1 - c, pr_cross)

    def send_part(j, carry):
        w_local(j).wait()
        w_remote(j).wait_recv()
        p0buf[j] = project(0, j).astype(bf16)
        y_copy(j).start()
        return carry

    lax.fori_loop(0, NCH, send_part, 0)

    a_wait(1, 0, 1 - c, sib_dev)
    a_wait(1, 1, c, pr_dev)
    a_wait(1, 1, 1 - c, pr_cross)

    def own_part(j, carry):
        p1buf[j] = project(1, j)
        return carry

    lax.fori_loop(0, NCH, own_part, 0)

    mine = pl.multiple_of(e * 64, 64)
    other = pl.multiple_of((1 - e) * 64, 64)

    def xh_copy(block_is_own, j):
        n = 0 if block_is_own else 1
        device = e_dev if block_is_own else e_cross
        return remote(
            xsend.at[n, j], xrec.at[c, j], xh_send.at[n, j], xh_recv.at[c, j], device
        )

    def sb_copy(j):
        return remote(ssend.at[j], srec.at[j], sb_send.at[j], sb_recv.at[j], sib_dev)

    def after_y(j, carry):
        y_copy(j).wait_recv()
        p1buf[j] = p1buf[j] + prec[j].astype(f32)
        own_base = c * QT
        sib_base = (1 - c) * QT
        xsend[0, j] = p1buf[j, pl.ds(pl.multiple_of(own_base + other, 64), 64), :].astype(bf16)
        xh_copy(True, j).start()
        xsend[1, j] = p1buf[j, pl.ds(pl.multiple_of(sib_base + other, 64), 64), :].astype(bf16)
        xh_copy(False, j).start()
        ssend[j] = p1buf[j, pl.ds(pl.multiple_of(sib_base + mine, 64), 64), :].astype(bf16)
        sb_copy(j).start()
        return carry

    lax.fori_loop(0, NCH, after_y, 0)

    res_copy.wait()

    def xh_wait(source_range, j):
        ref = xrec.at[source_range, j]
        remote(ref, ref, xh_send.at[0, j], xh_recv.at[source_range, j], e_dev).wait_recv()

    def finish(j, squares):
        xh_wait(c, j)
        cols = w_cols(j)
        kept_rows = pl.ds(pl.multiple_of(c * QT + mine, 64), 64)
        value = p1buf[j, kept_rows, :] + xrec[c, j].astype(f32) + resbuf[:, cols].astype(f32)
        comb[:, cols] = value
        stream_ref[:, cols] = value.astype(bf16)
        squares = squares + jnp.sum(value * value, axis=1, keepdims=True)
        xh_wait(1 - c, j)
        sb_copy(j).wait_recv()
        cols = pl.ds(pl.multiple_of((1 - c) * HALF + j * CC, 128), CC)
        value = srec[j].astype(f32) + xrec[1 - c, j].astype(f32) + resbuf[:, cols].astype(f32)
        comb[:, cols] = value
        stream_ref[:, cols] = value.astype(bf16)
        return squares + jnp.sum(value * value, axis=1, keepdims=True)

    squares = lax.fori_loop(0, NCH, finish, jnp.zeros((64, 1), f32))
    factor = lax.rsqrt(squares / D + 1e-05)

    def normalise(j, carry):
        cols = pl.ds(pl.multiple_of(j * CC, 128), CC)
        normed_ref[:, cols] = (comb[:, cols] * factor * gain_ref[:, cols].astype(f32)).astype(bf16)
        return carry

    lax.fori_loop(0, 2 * NCH, normalise, 0)

    @pl.when(h == 0)
    def _():
        anchor(0).wait_send()
        anchor(1).wait_send()

    x_copy().wait_send()
    for direction in range(2):
        for d in range(4):
            for x_ in range(2):
                if d < 3 or x_ == direction:
                    z_copy(direction, d, z, x_).wait_send()
    for g in range(8):
        for x_ in range(2):
            s_copy(g, z, x_).wait_send()
    for j in range(NCH):
        w_remote(j).wait_send()
        y_copy(j).wait_send()
        xh_copy(True, j).wait_send()
        xh_copy(False, j).wait_send()
        sb_copy(j).wait_send()
    for copy in a_copies():
        copy.wait_send()


def on_device(queries, key_states, value_states, passing, out_weight, residual, norm_gain):
    vmem = pl.BlockSpec(memory_space=pltpu.VMEM)
    anywhere = pl.BlockSpec(memory_space=pl.ANY)
    dma = pltpu.SemaphoreType.DMA
    out = jax.ShapeDtypeStruct((64, D), bf16)
    return pl.pallas_call(
        kernel,
        out_shape=(out, out),
        in_specs=[vmem, vmem, vmem, vmem, anywhere, anywhere, vmem],
        out_specs=(vmem, vmem),
        scratch_shapes=[
            pltpu.VMEM((8, 2, 2, 2, RET, HEAD), bf16),
            pltpu.VMEM((4, HEADS * QT, 2 * HEAD), bf16),
            pltpu.VMEM((HEADS * BLK, 2 * HEAD), f32),
            pltpu.VMEM((HEADS * BLK, HEAD), f32),
            pltpu.VMEM((NCH, 2 * BLK, CC), bf16),
            pltpu.VMEM((2, 2, 2, QT, BLK), bf16),
            pltpu.VMEM((2, QT, BLK), bf16),
            pltpu.VMEM((NCH, 2 * QT, CC), bf16),
            pltpu.VMEM((NCH, 2 * QT, CC), bf16),
            pltpu.VMEM((NCH, 2 * QT, CC), f32),
            pltpu.VMEM((2, NCH, 64, CC), bf16),
            pltpu.VMEM((2, NCH, 64, CC), bf16),
            pltpu.VMEM((NCH, 64, CC), bf16),
            pltpu.VMEM((NCH, 64, CC), bf16),
            pltpu.VMEM((64, D), f32),
            pltpu.VMEM((64, D), bf16),
            dma((2,)),
            dma((2,)),
            dma((1,)),
            dma((1,)),
            dma((2, 4, 2)),
            dma((2, 4, 2)),
            dma((8, 2)),
            dma((8, 2)),
            dma((NCH,)),
            dma((NCH,)),
            dma((NCH,)),
            dma((6,)),
            dma((2, 2, 2)),
            dma((NCH,)),
            dma((NCH,)),
            dma((2, NCH)),
            dma((2, NCH)),
            dma((NCH,)),
            dma((NCH,)),
            dma,
        ],
        compiler_params=pltpu.CompilerParams(
            collective_id=0, has_side_effects=True, vmem_limit_bytes=58 << 20
        ),
        name="layer",
    )(
        queries,
        key_states,
        value_states,
        passing,
        out_weight,
        residual,
        norm_gain.reshape(1, D),
    )


def solution(mesh):
    placed = (
        P("hst", "tp"),
        P("hst", "tp"),
        P("hst", "tp"),
        P("hst", None),
        P("tp", None),
        P(("hst", "tp"), None),
        P(),
    )
    return jax.shard_map(
        on_device,
        mesh=mesh,
        in_specs=placed,
        out_specs=(P(("hst", "tp"), None), P(("hst", "tp"), None)),
        check_vma=False,
    )
```

```python
import math

import jax
import jax.numpy as jnp
from jax import lax
from jax.experimental import pallas as pl
from jax.experimental.pallas import tpu as pltpu
from jax.sharding import PartitionSpec as P

f32 = jnp.float32
bf16 = jnp.bfloat16
MESH = pl.DeviceIdType.MESH

HEAD = 128
HEADS = 4
BLK = 512
RET = 256
D = 7168
HALF = D // 2
CC = 512
NCH = HALF // CC
SHARED = 4
QT = 128
LAST = 31
SCALE = math.log2(math.e) / math.sqrt(HEAD)
ROWS = 256
TILES = HEADS * BLK // ROWS
GKEYS = 4 * RET


def kernel(
    q_hbm,
    k_hbm,
    v_hbm,
    pass_ref,
    w_ref,
    res_ref,
    comb,
    kvbuf,
    qs,
    acc,
    peak,
    wall,
    abuf,
    ast,
    p0buf,
    prec,
    p1buf,
    xsend,
    xrec,
    ssend,
    srec,
    resbuf,
    q_ref,
    k_ref,
    v_ref,
    in_sem,
    an_send,
    an_recv,
    x_send,
    x_recv,
    z_send,
    z_recv,
    s_send,
    s_recv,
    wl_sem,
    w_send,
    w_recv,
    wf_send,
    wf_recv,
    a_send,
    a_recv,
    y_send,
    y_recv,
    xh_send,
    xh_recv,
    sb_send,
    sb_recv,
    res_sem,
):
    h = lax.axis_index("hst")
    t = lax.axis_index("tp")
    x = h // 16
    z = (h // 2) % 8
    c = h % 2
    y = t // 2
    e = t % 2
    turn = 1 - 2 * (y % 2)
    pr = (y + turn + 2 * c + 4) % 4
    nb = (y + turn + 2 * (1 - c) + 4) % 4

    def dev(x_, z_, c_, y_, e_):
        return (x_ * 16 + z_ * 2 + c_, y_ * 2 + e_)

    x_dev = dev(1 - x, z, c, y, e)
    up_dev = dev(x, (z + 1) % 8, c, y, e)
    down_dev = dev(x, (z + 7) % 8, c, y, e)
    sib_dev = dev(x, z, 1 - c, y, e)
    pr_dev = dev(x, z, c, pr, e)
    pr_cross = dev(x, z, 1 - c, pr, e)
    nb_dev = dev(x, z, c, nb, e)
    nb_cross = dev(x, z, 1 - c, nb, e)
    e_dev = dev(x, z, c, y, 1 - e)
    e_cross = dev(x, z, 1 - c, y, 1 - e)
    partners = (
        x_dev,
        up_dev,
        down_dev,
        sib_dev,
        pr_dev,
        pr_cross,
        nb_dev,
        nb_cross,
        e_dev,
        e_cross,
    )

    def remote(src, dst, send, recv, device):
        return pltpu.make_async_remote_copy(
            src_ref=src,
            dst_ref=dst,
            send_sem=send,
            recv_sem=recv,
            device_id=device,
            device_id_type=MESH,
        )

    col0 = c * HALF

    def w_cols(j):
        return pl.ds(pl.multiple_of(col0 + j * CC, 128), CC)

    def w_local(j):
        return pltpu.make_async_copy(
            w_ref.at[:, w_cols(j)], wall.at[j, pl.ds(0, BLK), :], wl_sem.at[j]
        )

    def w_half(j):
        rows = pl.ds(pl.multiple_of(x * RET, RET), RET)
        there = pl.ds(pl.multiple_of(BLK + x * RET, RET), RET)
        return remote(
            w_ref.at[rows, w_cols(j)],
            wall.at[j, there, :],
            w_send.at[j],
            w_recv.at[j],
            pr_dev,
        )

    def w_whole(j):
        return remote(
            w_ref.at[:, w_cols(j)],
            wall.at[j, pl.ds(BLK, BLK), :],
            w_send.at[j],
            w_recv.at[j],
            pr_dev,
        )

    def w_across(j, x_):
        there = wall.at[j, pl.ds(pl.multiple_of(BLK + x_ * RET, RET), RET), :]
        return remote(there, there, wf_send.at[j], wf_recv.at[j], x_dev)

    res_copy = pltpu.make_async_copy(res_ref, resbuf, res_sem)

    loads = (
        pltpu.make_async_copy(k_hbm, k_ref, in_sem.at[0]),
        pltpu.make_async_copy(v_hbm, v_ref, in_sem.at[1]),
        pltpu.make_async_copy(q_hbm, q_ref, in_sem.at[2]),
    )
    for load in loads:
        load.start()

    barrier = pltpu.get_barrier_semaphore()
    for partner in partners:
        pl.semaphore_signal(barrier, inc=1, device_id=partner, device_id_type=MESH)

    @pl.when(h == 0)
    def _():
        pl.semaphore_signal(barrier, inc=1, device_id=(LAST, t), device_id_type=MESH)

    @pl.when(h == LAST)
    def _():
        pl.semaphore_signal(barrier, inc=1, device_id=(0, t), device_id_type=MESH)

    loads[0].wait()
    loads[1].wait()
    lane = lax.broadcasted_iota(jnp.int32, (BLK, RET), 1)
    sub = lax.broadcasted_iota(jnp.int32, (BLK, RET), 0)
    chosen = jnp.where(h == 0, lane, jnp.broadcast_to(pass_ref[...], (BLK, RET)))
    onehot = (sub == chosen).astype(bf16)
    both = jnp.concatenate([k_ref[...], v_ref[...]], axis=1)
    kept = lax.dot_general(
        onehot, both, (((0,), (0,)), ((), ())), preferred_element_type=f32
    ).astype(bf16)

    @pl.when(h != LAST)
    def _():
        kvbuf[z, c, x, 0] = kept[:, :HEAD]
        kvbuf[z, c, x, 1] = kept[:, HEAD:]

    extra = jnp.where((h == 0) | (h == LAST), 1, 0)
    pl.semaphore_wait(barrier, len(partners) + extra)

    def anchor(i):
        src = (k_ref, v_ref)[i].at[pl.ds(RET, RET), :]
        return remote(src, kvbuf.at[7, 1, 1, i], an_send.at[i], an_recv.at[i], (LAST, t))

    def anchor_in(i):
        src = (k_ref, v_ref)[i].at[pl.ds(RET, RET), :]
        return remote(src, kvbuf.at[7, 1, 1, i], an_send.at[i], an_recv.at[i], (0, t))

    @pl.when(h == 0)
    def _():
        anchor(0).start()
        anchor(1).start()

    @pl.when(h == LAST)
    def _():
        anchor_in(0).wait_recv()
        anchor_in(1).wait_recv()

    def slot(z_, x_):
        return kvbuf.at[z_, c, x_]

    def x_copy():
        return remote(slot(z, x), slot(z, x), x_send.at[0], x_recv.at[0], x_dev)

    def z_copy(direction, d, z_, x_):
        device = up_dev if direction == 0 else down_dev
        return remote(
            slot(z_, x_),
            slot(z_, x_),
            z_send.at[direction, d, x_],
            z_recv.at[direction, d, x_],
            device,
        )

    def s_copy(g, z_, x_, i):
        return remote(slot(z_, x_), slot(z_, x_), s_send.at[g, i], s_recv.at[g, i], sib_dev)

    def s_wait(g, z_, x_, i):
        theirs = kvbuf.at[z_, 1 - c, x_]
        remote(theirs, theirs, s_send.at[g, i], s_recv.at[g, i], sib_dev).wait_recv()

    x_copy().start()
    z_copy(0, 0, z, x).start()
    z_copy(1, 0, z, x).start()
    s_copy(0, z, x, x).start()
    for j in range(SHARED):
        w_half(j).start()
    for j in range(SHARED, NCH):
        w_whole(j).start()
    for j in range(NCH):
        w_local(j).start()
    res_copy.start()

    loads[2].wait()
    quarters = ((y + 2) % 4, pr, nb, y)
    for r in range(4):
        rows = pl.ds(pl.multiple_of(quarters[r] * QT, QT), QT)
        for head in range(HEADS):
            scaled = q_ref[rows, head * HEAD : (head + 1) * HEAD].astype(f32) * SCALE
            high = scaled.astype(bf16)
            low = (scaled - high.astype(f32)).astype(bf16)
            qs[r, head * QT : (head + 1) * QT, :HEAD] = high
            qs[r, head * QT : (head + 1) * QT, HEAD:] = low

    def logits(tile, keys2):
        r, half = tile // 2, tile % 2
        return lax.dot_general(
            qs[r, half * ROWS : (half + 1) * ROWS, :],
            keys2,
            (((1,), (1,)), ((), ())),
            preferred_element_type=f32,
        )

    own_keys = jnp.concatenate([k_ref[...], k_ref[...]], axis=1)
    own_values = jnp.concatenate([v_ref[...], jnp.ones((BLK, HEAD), bf16)], axis=1)
    key_at = lax.broadcasted_iota(jnp.int32, (ROWS, BLK), 1)
    row_at = lax.broadcasted_iota(jnp.int32, (ROWS, BLK), 0) % QT
    for tile in range(TILES):
        scores = logits(tile, own_keys)
        seen = key_at <= row_at + quarters[tile // 2] * QT
        scores = jnp.where(seen, scores, -jnp.inf)
        newest = jnp.max(scores, axis=1, keepdims=True)
        weights = jnp.exp2(scores - newest).astype(bf16)
        rows = pl.ds(tile * ROWS, ROWS)
        peak[rows, :] = jnp.broadcast_to(newest, (ROWS, HEAD))
        acc[rows, :] = jnp.dot(weights, own_values, preferred_element_type=f32)

    x_copy().wait_recv()
    z_copy(0, 0, z, 1 - x).start()
    z_copy(1, 0, z, 1 - x).start()
    s_copy(0, z, 1 - x, 1 - x).start()

    first_key = k_ref[0:1, :]

    def place(g, i):
        inner = (g >= 1) & (g <= 6)
        d = (g + 1) // 2
        turned = (z + 8 - d + 2 * d * i) % 8
        z_ = jnp.where(inner, turned, (z + jnp.where(g == 7, 4, 0)) % 8)
        x_ = jnp.where(inner, jnp.where(g % 2 == 1, x, 1 - x), i)
        return z_, x_

    def pass_on(g):
        d = (g + 1) // 2
        for i in range(2):
            z_, x_ = place(g, i)
            z_copy(i, d - 1, z_, x_).wait_recv()

            @pl.when((d < 3) | (x_ == i))
            def _():
                z_copy(i, d, z_, x_).start()

            s_copy(g, z_, x_, i).start()

    def take_last():
        for i in range(2):
            z_, x_ = place(7, i)
            z_copy(i, 3, z_, x_).wait_recv()
            s_copy(7, z_, x_, i).start()

    def shown_in(number):
        return (number < h) | ((number == LAST) & (h >= 1))

    def load_group(g):
        key_parts, value_parts, unit_parts = [], [], []
        for i in range(2):
            z_, x_ = place(g, i)
            for c_ in range(2):
                shown = shown_in(x_ * 16 + z_ * 2 + c_)
                key_parts.append(jnp.where(shown, kvbuf[z_, c_, x_, 0], first_key))
                value_parts.append(
                    jnp.where(shown, kvbuf[z_, c_, x_, 1], jnp.zeros((RET, HEAD), bf16))
                )
                unit_parts.append(
                    jnp.where(shown, jnp.ones((RET, HEAD), bf16), jnp.zeros((RET, HEAD), bf16))
                )
        keys = jnp.concatenate(key_parts, axis=0)
        keys2 = jnp.concatenate([keys, keys], axis=1)
        values2 = jnp.concatenate(
            [jnp.concatenate(value_parts, axis=0), jnp.concatenate(unit_parts, axis=0)], axis=1
        )
        return keys2, values2

    def absorb(tile, scores, values2):
        rows = pl.ds(tile * ROWS, ROWS)
        before = peak[rows, :]
        newest = jnp.maximum(before, jnp.max(scores, axis=1, keepdims=True))
        shrink = jnp.exp2(before - newest)
        peak[rows, :] = newest
        weights = jnp.exp2(scores - newest[:, :1]).astype(bf16)
        added = jnp.dot(weights, values2, preferred_element_type=f32)
        old = acc[rows, :]
        acc[rows, :] = (
            jnp.concatenate([old[:, :HEAD] * shrink, old[:, HEAD:] * shrink], axis=1) + added
        )

    def one_group(g, carry):
        @pl.when(g <= 5)
        def _():
            pass_on(g + 1)

        @pl.when(g == 6)
        def _():
            take_last()

        @pl.when((g >= 1) & (g <= SHARED))
        def _():
            w_half(g - 1).wait_recv()
            w_across(g - 1, x).start()

        used = False
        for i in range(2):
            z_, x_ = place(g, i)
            s_wait(g, z_, x_, i)
            for c_ in range(2):
                used = used | shown_in(x_ * 16 + z_ * 2 + c_)

        @pl.when(used)
        def _():
            keys2, values2 = load_group(g)
            all_scores = [logits(tile, keys2) for tile in range(TILES)]
            for tile in range(TILES):
                absorb(tile, all_scores[tile], values2)

        return carry

    lax.fori_loop(0, 7, one_group, 0)
    for i in range(2):
        z_, x_ = place(7, i)
        s_wait(7, z_, x_, i)

    def attended(r, put):
        for head in range(HEADS):
            rows = pl.ds(r * HEADS * QT + head * QT, QT)
            value = (acc[rows, :HEAD] / acc[rows, HEAD:]).astype(bf16)
            put(head, value)

    def put_ast(r):
        def put(head, value):
            ast[r, :, head * HEAD : (head + 1) * HEAD] = value

        return put

    def put_own(tok):
        def put(head, value):
            abuf[tok, 0, c, :, head * HEAD : (head + 1) * HEAD] = value

        return put

    def a_copy(n, src, tok, source, device):
        return remote(
            src, abuf.at[tok, source, c], a_send.at[n], a_recv.at[tok, source, c], device
        )

    def a_copies():
        return (
            a_copy(0, ast.at[0], 0, 1, pr_dev),
            a_copy(1, ast.at[0], 0, 1, nb_cross),
            a_copy(2, ast.at[1], 1, 1, pr_dev),
            a_copy(3, ast.at[1], 0, 0, sib_dev),
            a_copy(4, abuf.at[0, 0, c], 1, 1, nb_cross),
            a_copy(5, abuf.at[1, 0, c], 1, 0, sib_dev),
        )

    copies = a_copies()
    keys2, values2 = load_group(7)
    all_scores = [logits(tile, keys2) for tile in range(TILES)]
    puts = (put_ast(0), put_ast(1), put_own(0), put_own(1))
    sent = ((0, 1), (3, 2), (4,), (5,))
    for r in range(4):
        for tile in (2 * r, 2 * r + 1):
            absorb(tile, all_scores[tile], values2)
        attended(r, puts[r])
        for n in sent[r]:
            copies[n].start()

    def a_wait(tok, source, block, device):
        ref = abuf.at[tok, source, block]
        remote(ref, ref, a_send.at[0], a_recv.at[tok, source, block], device).wait_recv()

    def project(tok, j):
        total = None
        for source in range(2):
            rows = abuf[tok, source].reshape(2 * QT, BLK)
            term = jnp.dot(
                rows, wall[j, source * BLK : (source + 1) * BLK, :], preferred_element_type=f32
            )
            total = term if total is None else total + term
        return total

    def y_copy(j):
        return remote(p0buf.at[j], prec.at[j], y_send.at[j], y_recv.at[j], nb_dev)

    a_wait(0, 0, 1 - c, sib_dev)
    a_wait(0, 1, c, pr_dev)
    a_wait(0, 1, 1 - c, pr_cross)

    def send_part(j, carry):
        w_local(j).wait()

        @pl.when(j < SHARED)
        def _():
            w_across(j, 1 - x).wait_recv()

        @pl.when(j >= SHARED)
        def _():
            w_whole(j).wait_recv()

        p0buf[j] = project(0, j).astype(bf16)
        y_copy(j).start()
        return carry

    lax.fori_loop(0, NCH, send_part, 0)

    a_wait(1, 0, 1 - c, sib_dev)
    a_wait(1, 1, c, pr_dev)
    a_wait(1, 1, 1 - c, pr_cross)

    def own_part(j, carry):
        p1buf[j] = project(1, j)
        return carry

    lax.fori_loop(0, NCH, own_part, 0)

    mine = pl.multiple_of(e * 64, 64)
    other = pl.multiple_of((1 - e) * 64, 64)

    def xh_copy(block_is_own, j):
        n = 0 if block_is_own else 1
        device = e_dev if block_is_own else e_cross
        return remote(
            xsend.at[n, j], xrec.at[c, j], xh_send.at[n, j], xh_recv.at[c, j], device
        )

    def sb_copy(j):
        return remote(ssend.at[j], srec.at[j], sb_send.at[j], sb_recv.at[j], sib_dev)

    def after_y(j, carry):
        y_copy(j).wait_recv()
        p1buf[j] = p1buf[j] + prec[j].astype(f32)
        own_base = c * QT
        sib_base = (1 - c) * QT
        xsend[0, j] = p1buf[j, pl.ds(pl.multiple_of(own_base + other, 64), 64), :].astype(bf16)
        xh_copy(True, j).start()
        xsend[1, j] = p1buf[j, pl.ds(pl.multiple_of(sib_base + other, 64), 64), :].astype(bf16)
        xh_copy(False, j).start()
        ssend[j] = p1buf[j, pl.ds(pl.multiple_of(sib_base + mine, 64), 64), :].astype(bf16)
        sb_copy(j).start()
        return carry

    lax.fori_loop(0, NCH, after_y, 0)

    res_copy.wait()

    def xh_wait(source_range, j):
        ref = xrec.at[source_range, j]
        remote(ref, ref, xh_send.at[0, j], xh_recv.at[source_range, j], e_dev).wait_recv()

    def finish(j, carry):
        xh_wait(c, j)
        cols = w_cols(j)
        kept_rows = pl.ds(pl.multiple_of(c * QT + mine, 64), 64)
        value = p1buf[j, kept_rows, :] + xrec[c, j].astype(f32)
        comb[:, cols] = value + resbuf[:, cols].astype(f32)
        xh_wait(1 - c, j)
        sb_copy(j).wait_recv()
        cols = pl.ds(pl.multiple_of((1 - c) * HALF + j * CC, 128), CC)
        value = srec[j].astype(f32) + xrec[1 - c, j].astype(f32)
        comb[:, cols] = value + resbuf[:, cols].astype(f32)
        return carry

    lax.fori_loop(0, NCH, finish, 0)

    @pl.when(h == 0)
    def _():
        anchor(0).wait_send()
        anchor(1).wait_send()

    x_copy().wait_send()
    for direction in range(2):
        for d in range(4):
            for x_ in range(2):
                if d < 3 or x_ == direction:
                    z_copy(direction, d, z, x_).wait_send()
    for g in range(8):
        for x_ in range(2):
            s_copy(g, z, x_, x_).wait_send()
    for j in range(NCH):
        y_copy(j).wait_send()
        xh_copy(True, j).wait_send()
        xh_copy(False, j).wait_send()
        sb_copy(j).wait_send()
    for j in range(SHARED):
        w_half(j).wait_send()
        w_across(j, x).wait_send()
    for j in range(SHARED, NCH):
        w_whole(j).wait_send()
    for copy in a_copies():
        copy.wait_send()


def norm_kernel(comb, gain, stream_ref, normed_ref):
    value = comb[...]
    stream_ref[...] = value.astype(bf16)
    factor = lax.rsqrt(jnp.mean(value * value, axis=1, keepdims=True) + 1e-05)
    normed_ref[...] = (value * factor * gain[...].astype(f32)[None, :]).astype(bf16)


def on_device(queries, key_states, value_states, passing, out_weight, residual, norm_gain):
    vmem = pl.BlockSpec(memory_space=pltpu.VMEM)
    anywhere = pl.BlockSpec(memory_space=pl.ANY)
    dma = pltpu.SemaphoreType.DMA
    out = jax.ShapeDtypeStruct((64, D), bf16)
    combined = pl.pallas_call(
        kernel,
        out_shape=jax.ShapeDtypeStruct((64, D), f32),
        in_specs=[anywhere, anywhere, anywhere, vmem, anywhere, anywhere],
        out_specs=vmem,
        scratch_shapes=[
            pltpu.VMEM((8, 2, 2, 2, RET, HEAD), bf16),
            pltpu.VMEM((4, HEADS * QT, 2 * HEAD), bf16),
            pltpu.VMEM((HEADS * BLK, 2 * HEAD), f32),
            pltpu.VMEM((HEADS * BLK, HEAD), f32),
            pltpu.VMEM((NCH, 2 * BLK, CC), bf16),
            pltpu.VMEM((2, 2, 2, QT, BLK), bf16),
            pltpu.VMEM((2, QT, BLK), bf16),
            pltpu.VMEM((NCH, 2 * QT, CC), bf16),
            pltpu.VMEM((NCH, 2 * QT, CC), bf16),
            pltpu.VMEM((NCH, 2 * QT, CC), f32),
            pltpu.VMEM((2, NCH, 64, CC), bf16),
            pltpu.VMEM((2, NCH, 64, CC), bf16),
            pltpu.VMEM((NCH, 64, CC), bf16),
            pltpu.VMEM((NCH, 64, CC), bf16),
            pltpu.VMEM((64, D), bf16),
            pltpu.VMEM((BLK, HEADS * HEAD), bf16),
            pltpu.VMEM((BLK, HEAD), bf16),
            pltpu.VMEM((BLK, HEAD), bf16),
            dma((3,)),
            dma((2,)),
            dma((2,)),
            dma((1,)),
            dma((1,)),
            dma((2, 4, 2)),
            dma((2, 4, 2)),
            dma((8, 2)),
            dma((8, 2)),
            dma((NCH,)),
            dma((NCH,)),
            dma((NCH,)),
            dma((SHARED,)),
            dma((SHARED,)),
            dma((6,)),
            dma((2, 2, 2)),
            dma((NCH,)),
            dma((NCH,)),
            dma((2, NCH)),
            dma((2, NCH)),
            dma((NCH,)),
            dma((NCH,)),
            dma,
        ],
        compiler_params=pltpu.CompilerParams(
            collective_id=0, has_side_effects=True, vmem_limit_bytes=58 << 20
        ),
        name="layer",
    )(
        queries,
        key_states,
        value_states,
        passing,
        out_weight,
        residual,
    )
    return pl.pallas_call(
        norm_kernel,
        out_shape=(out, out),
        in_specs=[vmem, vmem],
        out_specs=(vmem, vmem),
        name="norm",
    )(combined, norm_gain)


def solution(mesh):
    placed = (
        P("hst", "tp"),
        P("hst", "tp"),
        P("hst", "tp"),
        P("hst", None),
        P("tp", None),
        P(("hst", "tp"), None),
        P(),
    )
    return jax.shard_map(
        on_device,
        mesh=mesh,
        in_specs=placed,
        out_specs=(P(("hst", "tp"), None), P(("hst", "tp"), None)),
        check_vma=False,
    )
```

```python
import math

import jax
import jax.numpy as jnp
from jax import lax
from jax.experimental import pallas as pl
from jax.experimental.pallas import tpu as pltpu
from jax.sharding import PartitionSpec as P

f32 = jnp.float32
bf16 = jnp.bfloat16
MESH = pl.DeviceIdType.MESH

HEAD = 128
HEADS = 4
BLK = 512
RET = 256
D = 7168
HALF = D // 2
CC = 512
BEHIND = 3
NCH = HALF // CC
SHARED = 4
SHARED_COLS = 512
WHOLE = 2
WHOLE_COLS = (HALF - SHARED * SHARED_COLS) // WHOLE
QT = 128
LAST = 31
SCALE = math.log2(math.e) / math.sqrt(HEAD)
ROWS = 256
TILES = HEADS * BLK // ROWS
GKEYS = 4 * RET


def kernel(
    q_hbm,
    k_hbm,
    v_hbm,
    pass_ref,
    w_ref,
    res_ref,
    comb,
    kvbuf,
    qs,
    acc,
    peak,
    wall,
    abuf,
    ast,
    p0buf,
    prec,
    p1buf,
    xsend,
    xrec,
    ssend,
    srec,
    resbuf,
    q_ref,
    k_ref,
    v_ref,
    in_sem,
    an_send,
    an_recv,
    x_send,
    x_recv,
    z_send,
    z_recv,
    s_send,
    s_recv,
    wl_sem,
    w_send,
    w_recv,
    wf_send,
    wf_recv,
    a_send,
    a_recv,
    y_send,
    y_recv,
    xh_send,
    xh_recv,
    sb_send,
    sb_recv,
    res_sem,
):
    h = lax.axis_index("hst")
    t = lax.axis_index("tp")
    x = h // 16
    z = (h // 2) % 8
    c = h % 2
    y = t // 2
    e = t % 2
    turn = 1 - 2 * (y % 2)
    pr = (y + turn + 2 * c + 4) % 4
    nb = (y + turn + 2 * (1 - c) + 4) % 4

    def dev(x_, z_, c_, y_, e_):
        return (x_ * 16 + z_ * 2 + c_, y_ * 2 + e_)

    x_dev = dev(1 - x, z, c, y, e)
    up_dev = dev(x, (z + 1) % 8, c, y, e)
    down_dev = dev(x, (z + 7) % 8, c, y, e)
    sib_dev = dev(x, z, 1 - c, y, e)
    pr_dev = dev(x, z, c, pr, e)
    pr_cross = dev(x, z, 1 - c, pr, e)
    nb_dev = dev(x, z, c, nb, e)
    nb_cross = dev(x, z, 1 - c, nb, e)
    e_dev = dev(x, z, c, y, 1 - e)
    e_cross = dev(x, z, 1 - c, y, 1 - e)
    partners = (
        x_dev,
        up_dev,
        down_dev,
        sib_dev,
        pr_dev,
        pr_cross,
        nb_dev,
        nb_cross,
        e_dev,
        e_cross,
    )

    def remote(src, dst, send, recv, device):
        return pltpu.make_async_remote_copy(
            src_ref=src,
            dst_ref=dst,
            send_sem=send,
            recv_sem=recv,
            device_id=device,
            device_id_type=MESH,
        )

    col0 = c * HALF

    def w_cols(j):
        return pl.ds(pl.multiple_of(col0 + j * CC, 128), CC)

    w_local = pltpu.make_async_copy(
        w_ref.at[:, pl.ds(pl.multiple_of(col0, 128), HALF)], wall.at[pl.ds(0, BLK), :], wl_sem
    )

    def w_unit(u):
        if u < SHARED:
            start, width, rows = u * SHARED_COLS, SHARED_COLS, RET
            first = pl.multiple_of(x * RET, RET)
        else:
            start, width, rows = SHARED * SHARED_COLS + (u - SHARED) * WHOLE_COLS, WHOLE_COLS, BLK
            first = 0
        return remote(
            w_ref.at[pl.ds(first, rows), pl.ds(pl.multiple_of(col0 + start, 128), width)],
            wall.at[pl.ds(BLK + first, rows), pl.ds(start, width)],
            w_send.at[u],
            w_recv.at[u],
            pr_dev,
        )

    def w_across(u, x_):
        first = pl.multiple_of(BLK + x_ * RET, RET)
        there = wall.at[pl.ds(first, RET), pl.ds(u * SHARED_COLS, SHARED_COLS)]
        return remote(there, there, wf_send.at[u], wf_recv.at[u], x_dev)

    res_copy = pltpu.make_async_copy(res_ref, resbuf, res_sem)

    loads = (
        pltpu.make_async_copy(k_hbm, k_ref, in_sem.at[0]),
        pltpu.make_async_copy(v_hbm, v_ref, in_sem.at[1]),
        pltpu.make_async_copy(q_hbm, q_ref, in_sem.at[2]),
    )
    for load in loads:
        load.start()
    w_local.start()
    res_copy.start()

    barrier = pltpu.get_barrier_semaphore()
    for partner in partners:
        pl.semaphore_signal(barrier, inc=1, device_id=partner, device_id_type=MESH)

    @pl.when(h == 0)
    def _():
        pl.semaphore_signal(barrier, inc=1, device_id=(LAST, t), device_id_type=MESH)

    @pl.when(h == LAST)
    def _():
        pl.semaphore_signal(barrier, inc=1, device_id=(0, t), device_id_type=MESH)

    loads[0].wait()
    loads[1].wait()
    lane = lax.broadcasted_iota(jnp.int32, (BLK, RET), 1)
    sub = lax.broadcasted_iota(jnp.int32, (BLK, RET), 0)
    chosen = jnp.where(h == 0, lane, jnp.broadcast_to(pass_ref[...], (BLK, RET)))
    onehot = (sub == chosen).astype(bf16)
    both = jnp.concatenate([k_ref[...], v_ref[...]], axis=1)
    kept = lax.dot_general(
        onehot, both, (((0,), (0,)), ((), ())), preferred_element_type=f32
    ).astype(bf16)

    @pl.when(h != LAST)
    def _():
        kvbuf[z, c, x, 0] = kept[:, :HEAD]
        kvbuf[z, c, x, 1] = kept[:, HEAD:]

    loads[2].wait()
    quarters = ((y + 2) % 4, pr, nb, y)
    for r in range(4):
        rows = pl.ds(pl.multiple_of(quarters[r] * QT, QT), QT)
        for head in range(HEADS):
            scaled = q_ref[rows, head * HEAD : (head + 1) * HEAD].astype(f32) * SCALE
            high = scaled.astype(bf16)
            low = (scaled - high.astype(f32)).astype(bf16)
            qs[r, head * QT : (head + 1) * QT, :HEAD] = high
            qs[r, head * QT : (head + 1) * QT, HEAD:] = low

    extra = jnp.where((h == 0) | (h == LAST), 1, 0)
    pl.semaphore_wait(barrier, len(partners) + extra)

    def anchor(i):
        src = (k_ref, v_ref)[i].at[pl.ds(RET, RET), :]
        return remote(src, kvbuf.at[7, 1, 1, i], an_send.at[i], an_recv.at[i], (LAST, t))

    def anchor_in(i):
        src = (k_ref, v_ref)[i].at[pl.ds(RET, RET), :]
        return remote(src, kvbuf.at[7, 1, 1, i], an_send.at[i], an_recv.at[i], (0, t))

    @pl.when(h == 0)
    def _():
        anchor(0).start()
        anchor(1).start()

    @pl.when(h == LAST)
    def _():
        anchor_in(0).wait_recv()
        anchor_in(1).wait_recv()

    def slot(z_, x_):
        return kvbuf.at[z_, c, x_]

    def x_copy():
        return remote(slot(z, x), slot(z, x), x_send.at[0], x_recv.at[0], x_dev)

    def z_copy(direction, d, z_, x_):
        device = up_dev if direction == 0 else down_dev
        return remote(
            slot(z_, x_),
            slot(z_, x_),
            z_send.at[direction, d, x_],
            z_recv.at[direction, d, x_],
            device,
        )

    def s_copy(g, z_, x_, i):
        return remote(slot(z_, x_), slot(z_, x_), s_send.at[g, i], s_recv.at[g, i], sib_dev)

    def s_wait(g, z_, x_, i):
        theirs = kvbuf.at[z_, 1 - c, x_]
        remote(theirs, theirs, s_send.at[g, i], s_recv.at[g, i], sib_dev).wait_recv()

    x_copy().start()
    z_copy(0, 0, z, x).start()
    z_copy(1, 0, z, x).start()
    s_copy(0, z, x, x).start()
    for u in range(SHARED + WHOLE):
        w_unit(u).start()

    def logits(tile, keys2):
        r, half = tile // 2, tile % 2
        return lax.dot_general(
            qs[r, half * ROWS : (half + 1) * ROWS, :],
            keys2,
            (((1,), (1,)), ((), ())),
            preferred_element_type=f32,
        )

    own_keys = jnp.concatenate([k_ref[...], k_ref[...]], axis=1)
    own_values = jnp.concatenate([v_ref[...], jnp.ones((BLK, HEAD), bf16)], axis=1)
    key_at = lax.broadcasted_iota(jnp.int32, (ROWS, BLK), 1)
    row_at = lax.broadcasted_iota(jnp.int32, (ROWS, BLK), 0) % QT
    for tile in range(TILES):
        scores = logits(tile, own_keys)
        seen = key_at <= row_at + quarters[tile // 2] * QT
        scores = jnp.where(seen, scores, -jnp.inf)
        newest = jnp.max(scores, axis=1, keepdims=True)
        weights = jnp.exp2(scores - newest).astype(bf16)
        rows = pl.ds(tile * ROWS, ROWS)
        peak[rows, :] = jnp.broadcast_to(newest, (ROWS, HEAD))
        acc[rows, :] = jnp.dot(weights, own_values, preferred_element_type=f32)

    x_copy().wait_recv()
    z_copy(0, 0, z, 1 - x).start()
    z_copy(1, 0, z, 1 - x).start()
    s_copy(0, z, 1 - x, 1 - x).start()

    first_key = k_ref[0:1, :]

    def place(g, i):
        inner = (g >= 1) & (g <= 6)
        d = (g + 1) // 2
        turned = (z + 8 - d + 2 * d * i) % 8
        z_ = jnp.where(inner, turned, (z + jnp.where(g == 7, 4, 0)) % 8)
        x_ = jnp.where(inner, jnp.where(g % 2 == 1, x, 1 - x), i)
        return z_, x_

    def pass_on(g):
        d = (g + 1) // 2
        for i in range(2):
            z_, x_ = place(g, i)
            z_copy(i, d - 1, z_, x_).wait_recv()

            @pl.when((d < 3) | (x_ != i))
            def _():
                z_copy(i, d, z_, x_).start()

            s_copy(g, z_, x_, i).start()

    def take_last():
        for i in range(2):
            z_, x_ = place(7, i)
            z_copy(1 - i, 3, z_, x_).wait_recv()
            s_copy(7, z_, x_, i).start()

    def shown_in(number):
        return (number < h) | ((number == LAST) & (h >= 1))

    def load_group(g):
        key_parts, value_parts, unit_parts = [], [], []
        for i in range(2):
            z_, x_ = place(g, i)
            for c_ in range(2):
                shown = shown_in(x_ * 16 + z_ * 2 + c_)
                key_parts.append(jnp.where(shown, kvbuf[z_, c_, x_, 0], first_key))
                value_parts.append(
                    jnp.where(shown, kvbuf[z_, c_, x_, 1], jnp.zeros((RET, HEAD), bf16))
                )
                unit_parts.append(
                    jnp.where(shown, jnp.ones((RET, HEAD), bf16), jnp.zeros((RET, HEAD), bf16))
                )
        keys = jnp.concatenate(key_parts, axis=0)
        keys2 = jnp.concatenate([keys, keys], axis=1)
        values2 = jnp.concatenate(
            [jnp.concatenate(value_parts, axis=0), jnp.concatenate(unit_parts, axis=0)], axis=1
        )
        return keys2, values2

    def absorb(tile, scores, values2):
        rows = pl.ds(tile * ROWS, ROWS)
        before = peak[rows, :]
        newest = jnp.maximum(before, jnp.max(scores, axis=1, keepdims=True))
        shrink = jnp.exp2(before - newest)
        peak[rows, :] = newest
        weights = jnp.exp2(scores - newest[:, :1]).astype(bf16)
        added = jnp.dot(weights, values2, preferred_element_type=f32)
        old = acc[rows, :]
        acc[rows, :] = (
            jnp.concatenate([old[:, :HEAD] * shrink, old[:, HEAD:] * shrink], axis=1) + added
        )

    def one_group(g, carry):
        @pl.when(g <= 5)
        def _():
            pass_on(g + 1)

        @pl.when(g == 6)
        def _():
            take_last()

        for u in range(SHARED):

            @pl.when(g == u + 1)
            def _():
                w_unit(u).wait_recv()
                w_across(u, x).start()

        used = False
        for i in range(2):
            z_, x_ = place(g, i)
            s_wait(g, z_, x_, i)
            for c_ in range(2):
                used = used | shown_in(x_ * 16 + z_ * 2 + c_)

        @pl.when(used)
        def _():
            keys2, values2 = load_group(g)
            all_scores = [logits(tile, keys2) for tile in range(TILES)]
            for tile in range(TILES):
                absorb(tile, all_scores[tile], values2)

        return carry

    lax.fori_loop(0, 7, one_group, 0)
    for i in range(2):
        z_, x_ = place(7, i)
        s_wait(7, z_, x_, i)

    def attended(r, put):
        for head in range(HEADS):
            rows = pl.ds(r * HEADS * QT + head * QT, QT)
            value = (acc[rows, :HEAD] / acc[rows, HEAD:]).astype(bf16)
            put(head, value)

    def put_ast(r):
        def put(head, value):
            ast[r, :, head * HEAD : (head + 1) * HEAD] = value

        return put

    def put_own(tok):
        def put(head, value):
            abuf[tok, 0, c, :, head * HEAD : (head + 1) * HEAD] = value

        return put

    def a_copy(n, src, tok, source, device):
        return remote(
            src, abuf.at[tok, source, c], a_send.at[n], a_recv.at[tok, source, c], device
        )

    def a_copies():
        return (
            a_copy(0, ast.at[0], 0, 1, pr_dev),
            a_copy(1, ast.at[0], 0, 1, nb_cross),
            a_copy(2, ast.at[1], 1, 1, pr_dev),
            a_copy(3, ast.at[1], 0, 0, sib_dev),
            a_copy(4, abuf.at[0, 0, c], 1, 1, nb_cross),
            a_copy(5, abuf.at[1, 0, c], 1, 0, sib_dev),
        )

    copies = a_copies()
    keys2, values2 = load_group(7)
    all_scores = [logits(tile, keys2) for tile in range(TILES)]
    puts = (put_ast(0), put_ast(1), put_own(0), put_own(1))
    sent = ((0, 1), (3, 2), (4,), (5,))
    for r in range(4):
        for tile in (2 * r, 2 * r + 1):
            absorb(tile, all_scores[tile], values2)
        attended(r, puts[r])
        for n in sent[r]:
            copies[n].start()

    def a_wait(tok, source, block, device):
        ref = abuf.at[tok, source, block]
        remote(ref, ref, a_send.at[0], a_recv.at[tok, source, block], device).wait_recv()

    def project(tok, j):
        total = None
        for source in range(2):
            rows = abuf[tok, source].reshape(2 * QT, BLK)
            term = jnp.dot(
                rows,
                wall[source * BLK : (source + 1) * BLK, pl.ds(pl.multiple_of(j * CC, CC), CC)],
                preferred_element_type=f32,
            )
            total = term if total is None else total + term
        return total

    def y_copy(j):
        return remote(p0buf.at[j], prec.at[j], y_send.at[j], y_recv.at[j], nb_dev)

    a_wait(0, 0, 1 - c, sib_dev)
    a_wait(0, 1, c, pr_dev)
    a_wait(0, 1, 1 - c, pr_cross)

    def send_part(j, carry):
        for u in range(SHARED):

            @pl.when(j == u * SHARED_COLS // CC)
            def _():
                w_across(u, 1 - x).wait_recv()

        for u in range(WHOLE):

            @pl.when(j == (SHARED * SHARED_COLS + u * WHOLE_COLS) // CC)
            def _():
                w_unit(SHARED + u).wait_recv()

        p0buf[j] = project(0, j).astype(bf16)
        y_copy(j).start()
        return carry

    w_local.wait()
    lax.fori_loop(0, NCH, send_part, 0)

    a_wait(1, 0, 1 - c, sib_dev)
    a_wait(1, 1, c, pr_dev)
    a_wait(1, 1, 1 - c, pr_cross)

    def own_part(j, carry):
        p1buf[j] = project(1, j)
        return carry

    lax.fori_loop(0, NCH, own_part, 0)

    mine = pl.multiple_of(e * 64, 64)
    other = pl.multiple_of((1 - e) * 64, 64)

    def xh_copy(block_is_own, j):
        n = 0 if block_is_own else 1
        device = e_dev if block_is_own else e_cross
        return remote(
            xsend.at[n, j], xrec.at[c, j], xh_send.at[n, j], xh_recv.at[c, j], device
        )

    def sb_copy(j):
        return remote(ssend.at[j], srec.at[j], sb_send.at[j], sb_recv.at[j], sib_dev)

    def xh_wait(source_range, j):
        ref = xrec.at[source_range, j]
        remote(ref, ref, xh_send.at[0, j], xh_recv.at[source_range, j], e_dev).wait_recv()

    def finish(j):
        xh_wait(c, j)
        cols = w_cols(j)
        kept_rows = pl.ds(pl.multiple_of(c * QT + mine, 64), 64)
        value = p1buf[j, kept_rows, :] + xrec[c, j].astype(f32)
        comb[:, cols] = (value + resbuf[:, cols].astype(f32)).astype(bf16)
        xh_wait(1 - c, j)
        sb_copy(j).wait_recv()
        cols = pl.ds(pl.multiple_of((1 - c) * HALF + j * CC, 128), CC)
        value = srec[j].astype(f32) + xrec[1 - c, j].astype(f32)
        comb[:, cols] = (value + resbuf[:, cols].astype(f32)).astype(bf16)

    def after_y(j, carry):
        y_copy(j).wait_recv()

        def summed(first):
            rows = pl.ds(pl.multiple_of(first, 64), 64)
            return p1buf[j, rows, :] + prec[j, rows, :].astype(f32)

        own_base = c * QT
        sib_base = (1 - c) * QT
        xsend[0, j] = summed(own_base + other).astype(bf16)
        xh_copy(True, j).start()
        xsend[1, j] = summed(sib_base + other).astype(bf16)
        xh_copy(False, j).start()
        ssend[j] = summed(sib_base + mine).astype(bf16)
        sb_copy(j).start()
        p1buf[j, pl.ds(pl.multiple_of(own_base + mine, 64), 64), :] = summed(own_base + mine)

        @pl.when(j >= BEHIND)
        def _():
            finish(j - BEHIND)

        return carry

    res_copy.wait()
    lax.fori_loop(0, NCH, after_y, 0)
    for j in range(NCH - BEHIND, NCH):
        finish(j)

    @pl.when(h == 0)
    def _():
        anchor(0).wait_send()
        anchor(1).wait_send()

    x_copy().wait_send()
    for direction in range(2):
        for d in range(4):
            for x_ in range(2):
                if d < 3 or x_ != direction:
                    z_copy(direction, d, z, x_).wait_send()
    for g in range(8):
        for x_ in range(2):
            s_copy(g, z, x_, x_).wait_send()
    for j in range(NCH):
        y_copy(j).wait_send()
        xh_copy(True, j).wait_send()
        xh_copy(False, j).wait_send()
        sb_copy(j).wait_send()
    for u in range(SHARED + WHOLE):
        w_unit(u).wait_send()
    for j in range(SHARED):
        w_across(j, x).wait_send()
    for copy in a_copies():
        copy.wait_send()


def norm_kernel(comb, gain, stream_ref, normed_ref, normed, sems):
    keep = pltpu.make_async_copy(comb, stream_ref, sems.at[0])
    keep.start()
    value = comb[...].astype(f32)
    factor = lax.rsqrt(jnp.mean(value * value, axis=1, keepdims=True) + 1e-05)
    normed[...] = (value * factor * gain[...].astype(f32)[None, :]).astype(bf16)
    give = pltpu.make_async_copy(normed, normed_ref, sems.at[1])
    give.start()
    keep.wait()
    give.wait()


def on_device(queries, key_states, value_states, passing, out_weight, residual, norm_gain):
    vmem = pl.BlockSpec(memory_space=pltpu.VMEM)
    anywhere = pl.BlockSpec(memory_space=pl.ANY)
    dma = pltpu.SemaphoreType.DMA
    out = jax.ShapeDtypeStruct((64, D), bf16)
    combined = pl.pallas_call(
        kernel,
        out_shape=out,
        in_specs=[anywhere, anywhere, anywhere, vmem, anywhere, anywhere],
        out_specs=vmem,
        scratch_shapes=[
            pltpu.VMEM((8, 2, 2, 2, RET, HEAD), bf16),
            pltpu.VMEM((4, HEADS * QT, 2 * HEAD), bf16),
            pltpu.VMEM((HEADS * BLK, 2 * HEAD), f32),
            pltpu.VMEM((HEADS * BLK, HEAD), f32),
            pltpu.VMEM((2 * BLK, HALF), bf16),
            pltpu.VMEM((2, 2, 2, QT, BLK), bf16),
            pltpu.VMEM((2, QT, BLK), bf16),
            pltpu.VMEM((NCH, 2 * QT, CC), bf16),
            pltpu.VMEM((NCH, 2 * QT, CC), bf16),
            pltpu.VMEM((NCH, 2 * QT, CC), f32),
            pltpu.VMEM((2, NCH, 64, CC), bf16),
            pltpu.VMEM((2, NCH, 64, CC), bf16),
            pltpu.VMEM((NCH, 64, CC), bf16),
            pltpu.VMEM((NCH, 64, CC), bf16),
            pltpu.VMEM((64, D), bf16),
            pltpu.VMEM((BLK, HEADS * HEAD), bf16),
            pltpu.VMEM((BLK, HEAD), bf16),
            pltpu.VMEM((BLK, HEAD), bf16),
            dma((3,)),
            dma((2,)),
            dma((2,)),
            dma((1,)),
            dma((1,)),
            dma((2, 4, 2)),
            dma((2, 4, 2)),
            dma((8, 2)),
            dma((8, 2)),
            dma,
            dma((SHARED + WHOLE,)),
            dma((SHARED + WHOLE,)),
            dma((SHARED,)),
            dma((SHARED,)),
            dma((6,)),
            dma((2, 2, 2)),
            dma((NCH,)),
            dma((NCH,)),
            dma((2, NCH)),
            dma((2, NCH)),
            dma((NCH,)),
            dma((NCH,)),
            dma,
        ],
        compiler_params=pltpu.CompilerParams(
            collective_id=0, has_side_effects=True, vmem_limit_bytes=58 << 20
        ),
        name="layer",
    )(
        queries,
        key_states,
        value_states,
        passing,
        out_weight,
        residual,
    )
    return pl.pallas_call(
        norm_kernel,
        out_shape=(out, out),
        in_specs=[vmem, vmem],
        out_specs=(anywhere, anywhere),
        scratch_shapes=[pltpu.VMEM((64, D), bf16), dma((2,))],
        name="norm",
    )(combined, norm_gain)


def solution(mesh):
    placed = (
        P("hst", "tp"),
        P("hst", "tp"),
        P("hst", "tp"),
        P("hst", None),
        P("tp", None),
        P(("hst", "tp"), None),
        P(),
    )
    return jax.shard_map(
        on_device,
        mesh=mesh,
        in_specs=placed,
        out_specs=(P(("hst", "tp"), None), P(("hst", "tp"), None)),
        check_vma=False,
    )
```

```python
import math

import jax
import jax.numpy as jnp
from jax import lax
from jax.experimental import pallas as pl
from jax.experimental.pallas import tpu as pltpu
from jax.sharding import PartitionSpec as P

f32 = jnp.float32
bf16 = jnp.bfloat16
MESH = pl.DeviceIdType.MESH

HEAD = 128
HEADS = 4
BLK = 512
RET = 256
D = 7168
HALF = D // 2
CC = 512
BEHIND = 3
LOOK = 4
PART = 16
NCH = HALF // CC
SHARED = 4
SHARED_COLS = 512
WHOLE = 2
WHOLE_COLS = (HALF - SHARED * SHARED_COLS) // WHOLE
QT = 128
LAST = 31
SCALE = math.log2(math.e) / math.sqrt(HEAD)
ROWS = 256
TILES = HEADS * BLK // ROWS
GKEYS = 4 * RET


def kernel(
    q_hbm,
    k_hbm,
    v_hbm,
    pass_hbm,
    w_ref,
    res_ref,
    comb,
    kvbuf,
    qs,
    acc,
    peak,
    wall,
    abuf,
    ast,
    p0buf,
    prec,
    p1buf,
    xsend,
    xrec,
    ssend,
    srec,
    resbuf,
    q_ref,
    k_ref,
    v_ref,
    pass_ref,
    in_sem,
    an_send,
    an_recv,
    x_send,
    x_recv,
    z_send,
    z_recv,
    s_send,
    s_recv,
    wl_sem,
    w_send,
    w_recv,
    wf_send,
    wf_recv,
    a_send,
    a_recv,
    y_send,
    y_recv,
    xh_send,
    xh_recv,
    sb_send,
    sb_recv,
    res_sem,
):
    h = lax.axis_index("hst")
    t = lax.axis_index("tp")
    x = h // 16
    z = (h // 2) % 8
    c = h % 2
    y = t // 2
    e = t % 2
    turn = 1 - 2 * (y % 2)
    pr = (y + turn + 2 * c + 4) % 4
    nb = (y + turn + 2 * (1 - c) + 4) % 4

    def dev(x_, z_, c_, y_, e_):
        return (x_ * 16 + z_ * 2 + c_, y_ * 2 + e_)

    x_dev = dev(1 - x, z, c, y, e)
    up_dev = dev(x, (z + 1) % 8, c, y, e)
    down_dev = dev(x, (z + 7) % 8, c, y, e)
    sib_dev = dev(x, z, 1 - c, y, e)
    pr_dev = dev(x, z, c, pr, e)
    pr_cross = dev(x, z, 1 - c, pr, e)
    nb_dev = dev(x, z, c, nb, e)
    nb_cross = dev(x, z, 1 - c, nb, e)
    e_dev = dev(x, z, c, y, 1 - e)
    e_cross = dev(x, z, 1 - c, y, 1 - e)
    partners = (
        x_dev,
        up_dev,
        down_dev,
        sib_dev,
        pr_dev,
        pr_cross,
        nb_dev,
        nb_cross,
        e_dev,
        e_cross,
    )

    def remote(src, dst, send, recv, device):
        return pltpu.make_async_remote_copy(
            src_ref=src,
            dst_ref=dst,
            send_sem=send,
            recv_sem=recv,
            device_id=device,
            device_id_type=MESH,
        )

    col0 = c * HALF

    def w_cols(j):
        return pl.ds(pl.multiple_of(col0 + j * CC, 128), CC)

    w_local = pltpu.make_async_copy(
        w_ref.at[:, pl.ds(pl.multiple_of(col0, 128), HALF)], wall.at[pl.ds(0, BLK), :], wl_sem
    )

    def w_unit(u):
        if u < SHARED:
            start, width, rows = u * SHARED_COLS, SHARED_COLS, RET
            first = pl.multiple_of(x * RET, RET)
        else:
            start, width, rows = SHARED * SHARED_COLS + (u - SHARED) * WHOLE_COLS, WHOLE_COLS, BLK
            first = 0
        return remote(
            w_ref.at[pl.ds(first, rows), pl.ds(pl.multiple_of(col0 + start, 128), width)],
            wall.at[pl.ds(BLK + first, rows), pl.ds(start, width)],
            w_send.at[u],
            w_recv.at[u],
            pr_dev,
        )

    def w_across(u, x_):
        first = pl.multiple_of(BLK + x_ * RET, RET)
        there = wall.at[pl.ds(first, RET), pl.ds(u * SHARED_COLS, SHARED_COLS)]
        return remote(there, there, wf_send.at[u], wf_recv.at[u], x_dev)

    res_copy = pltpu.make_async_copy(res_ref, resbuf, res_sem)

    loads = (
        pltpu.make_async_copy(k_hbm, k_ref, in_sem.at[0]),
        pltpu.make_async_copy(v_hbm, v_ref, in_sem.at[1]),
        pltpu.make_async_copy(q_hbm, q_ref, in_sem.at[2]),
        pltpu.make_async_copy(pass_hbm, pass_ref, in_sem.at[3]),
    )
    for load in loads:
        load.start()
    w_local.start()
    res_copy.start()

    barrier = pltpu.get_barrier_semaphore()
    for partner in partners:
        pl.semaphore_signal(barrier, inc=1, device_id=partner, device_id_type=MESH)

    @pl.when(h == 0)
    def _():
        pl.semaphore_signal(barrier, inc=1, device_id=(LAST, t), device_id_type=MESH)

    @pl.when(h == LAST)
    def _():
        pl.semaphore_signal(barrier, inc=1, device_id=(0, t), device_id_type=MESH)

    loads[0].wait()
    loads[1].wait()
    loads[3].wait()
    lane = lax.broadcasted_iota(jnp.int32, (BLK, RET), 1)
    sub = lax.broadcasted_iota(jnp.int32, (BLK, RET), 0)
    chosen = jnp.where(h == 0, lane, jnp.broadcast_to(pass_ref[...], (BLK, RET)))
    onehot = (sub == chosen).astype(bf16)
    both = jnp.concatenate([k_ref[...], v_ref[...]], axis=1)
    kept = lax.dot_general(
        onehot, both, (((0,), (0,)), ((), ())), preferred_element_type=f32
    ).astype(bf16)

    @pl.when(h != LAST)
    def _():
        kvbuf[z, c, x, 0] = kept[:, :HEAD]
        kvbuf[z, c, x, 1] = kept[:, HEAD:]

    loads[2].wait()
    quarters = ((y + 2) % 4, pr, nb, y)
    for r in range(4):
        rows = pl.ds(pl.multiple_of(quarters[r] * QT, QT), QT)
        for head in range(HEADS):
            scaled = q_ref[rows, head * HEAD : (head + 1) * HEAD].astype(f32) * SCALE
            high = scaled.astype(bf16)
            low = (scaled - high.astype(f32)).astype(bf16)
            qs[r, head * QT : (head + 1) * QT, :HEAD] = high
            qs[r, head * QT : (head + 1) * QT, HEAD:] = low

    extra = jnp.where((h == 0) | (h == LAST), 1, 0)
    pl.semaphore_wait(barrier, len(partners) + extra)

    def anchor(i):
        src = (k_ref, v_ref)[i].at[pl.ds(RET, RET), :]
        return remote(src, kvbuf.at[7, 1, 1, i], an_send.at[i], an_recv.at[i], (LAST, t))

    def anchor_in(i):
        src = (k_ref, v_ref)[i].at[pl.ds(RET, RET), :]
        return remote(src, kvbuf.at[7, 1, 1, i], an_send.at[i], an_recv.at[i], (0, t))

    @pl.when(h == 0)
    def _():
        anchor(0).start()
        anchor(1).start()

    @pl.when(h == LAST)
    def _():
        anchor_in(0).wait_recv()
        anchor_in(1).wait_recv()

    def slot(z_, x_):
        return kvbuf.at[z_, c, x_]

    def x_copy():
        return remote(slot(z, x), slot(z, x), x_send.at[0], x_recv.at[0], x_dev)

    def z_copy(direction, d, z_, x_):
        device = up_dev if direction == 0 else down_dev
        return remote(
            slot(z_, x_),
            slot(z_, x_),
            z_send.at[direction, d, x_],
            z_recv.at[direction, d, x_],
            device,
        )

    def s_copy(g, z_, x_, i):
        return remote(slot(z_, x_), slot(z_, x_), s_send.at[g, i], s_recv.at[g, i], sib_dev)

    def s_wait(g, z_, x_, i):
        theirs = kvbuf.at[z_, 1 - c, x_]
        remote(theirs, theirs, s_send.at[g, i], s_recv.at[g, i], sib_dev).wait_recv()

    x_copy().start()
    z_copy(0, 0, z, x).start()
    z_copy(1, 0, z, x).start()
    s_copy(0, z, x, x).start()
    for u in range(SHARED + WHOLE):
        w_unit(u).start()

    def logits(tile, keys2):
        r, half = tile // 2, tile % 2
        return lax.dot_general(
            qs[r, half * ROWS : (half + 1) * ROWS, :],
            keys2,
            (((1,), (1,)), ((), ())),
            preferred_element_type=f32,
        )

    own_keys = jnp.concatenate([k_ref[...], k_ref[...]], axis=1)
    own_values = jnp.concatenate([v_ref[...], jnp.ones((BLK, HEAD), bf16)], axis=1)
    key_at = lax.broadcasted_iota(jnp.int32, (ROWS, BLK), 1)
    row_at = lax.broadcasted_iota(jnp.int32, (ROWS, BLK), 0) % QT
    own_scores = [logits(tile, own_keys) for tile in range(TILES)]
    for tile in range(TILES):
        scores = own_scores[tile]
        seen = key_at <= row_at + quarters[tile // 2] * QT
        scores = jnp.where(seen, scores, -jnp.inf)
        newest = jnp.max(scores, axis=1, keepdims=True)
        weights = jnp.exp2(scores - newest).astype(bf16)
        rows = pl.ds(tile * ROWS, ROWS)
        peak[rows, :] = jnp.broadcast_to(newest, (ROWS, HEAD))
        acc[rows, :] = jnp.dot(weights, own_values, preferred_element_type=f32)

    x_copy().wait_recv()
    z_copy(0, 0, z, 1 - x).start()
    z_copy(1, 0, z, 1 - x).start()
    s_copy(0, z, 1 - x, 1 - x).start()

    first_key = k_ref[0:1, :]

    def place(g, i):
        inner = (g >= 1) & (g <= 6)
        d = (g + 1) // 2
        turned = (z + 8 - d + 2 * d * i) % 8
        z_ = jnp.where(inner, turned, (z + jnp.where(g == 7, 4, 0)) % 8)
        x_ = jnp.where(inner, jnp.where(g % 2 == 1, x, 1 - x), i)
        return z_, x_

    def pass_on(g):
        d = (g + 1) // 2
        for i in range(2):
            z_, x_ = place(g, i)
            z_copy(i, d - 1, z_, x_).wait_recv()

            @pl.when((d < 3) | (x_ != i))
            def _():
                z_copy(i, d, z_, x_).start()

            s_copy(g, z_, x_, i).start()

    def take_last():
        for i in range(2):
            z_, x_ = place(7, i)
            z_copy(1 - i, 3, z_, x_).wait_recv()
            s_copy(7, z_, x_, i).start()

    def shown_in(number):
        return (number < h) | ((number == LAST) & (h >= 1))

    def load_group(g):
        key_parts, value_parts, unit_parts = [], [], []
        for i in range(2):
            z_, x_ = place(g, i)
            for c_ in range(2):
                shown = shown_in(x_ * 16 + z_ * 2 + c_)
                key_parts.append(jnp.where(shown, kvbuf[z_, c_, x_, 0], first_key))
                value_parts.append(
                    jnp.where(shown, kvbuf[z_, c_, x_, 1], jnp.zeros((RET, HEAD), bf16))
                )
                unit_parts.append(
                    jnp.where(shown, jnp.ones((RET, HEAD), bf16), jnp.zeros((RET, HEAD), bf16))
                )
        keys = jnp.concatenate(key_parts, axis=0)
        keys2 = jnp.concatenate([keys, keys], axis=1)
        values2 = jnp.concatenate(
            [jnp.concatenate(value_parts, axis=0), jnp.concatenate(unit_parts, axis=0)], axis=1
        )
        return keys2, values2

    def absorb(tile, scores, values2):
        rows = pl.ds(tile * ROWS, ROWS)
        before = peak[rows, :]
        newest = jnp.maximum(before, jnp.max(scores, axis=1, keepdims=True))
        shrink = jnp.exp2(before - newest)
        peak[rows, :] = newest
        weights = jnp.exp2(scores - newest[:, :1]).astype(bf16)
        added = jnp.dot(weights, values2, preferred_element_type=f32)
        old = acc[rows, :]
        acc[rows, :] = (
            jnp.concatenate([old[:, :HEAD] * shrink, old[:, HEAD:] * shrink], axis=1) + added
        )

    def one_group(g, carry):
        @pl.when(g <= 5)
        def _():
            pass_on(g + 1)

        @pl.when(g == 6)
        def _():
            take_last()

        for u in range(SHARED):

            @pl.when(g == u + 1)
            def _():
                w_unit(u).wait_recv()
                w_across(u, x).start()

        used = False
        for i in range(2):
            z_, x_ = place(g, i)
            s_wait(g, z_, x_, i)
            for c_ in range(2):
                used = used | shown_in(x_ * 16 + z_ * 2 + c_)

        @pl.when(used)
        def _():
            keys2, values2 = load_group(g)
            all_scores = [logits(tile, keys2) for tile in range(TILES)]
            for tile in range(TILES):
                absorb(tile, all_scores[tile], values2)

        return carry

    lax.fori_loop(0, 7, one_group, 0)
    for i in range(2):
        z_, x_ = place(7, i)
        s_wait(7, z_, x_, i)

    def attended(r, put):
        for head in range(HEADS):
            rows = pl.ds(r * HEADS * QT + head * QT, QT)
            value = (acc[rows, :HEAD] / acc[rows, HEAD:]).astype(bf16)
            put(head, value)

    def put_ast(r):
        def put(head, value):
            ast[r, :, head * HEAD : (head + 1) * HEAD] = value

        return put

    def put_own(tok):
        def put(head, value):
            abuf[tok, 0, c, :, head * HEAD : (head + 1) * HEAD] = value

        return put

    def a_copy(n, src, tok, source, device):
        return remote(
            src, abuf.at[tok, source, c], a_send.at[n], a_recv.at[tok, source, c], device
        )

    def a_copies():
        return (
            a_copy(0, ast.at[0], 0, 1, pr_dev),
            a_copy(1, ast.at[0], 0, 1, nb_cross),
            a_copy(2, ast.at[1], 1, 1, pr_dev),
            a_copy(3, ast.at[1], 0, 0, sib_dev),
            a_copy(4, abuf.at[0, 0, c], 1, 1, nb_cross),
            a_copy(5, abuf.at[1, 0, c], 1, 0, sib_dev),
        )

    copies = a_copies()
    keys2, values2 = load_group(7)
    all_scores = [logits(tile, keys2) for tile in range(LOOK)]
    puts = (put_ast(0), put_ast(1), put_own(0), put_own(1))
    sent = ((0, 1), (3, 2), (4,), (5,))
    for r in range(4):
        for tile in (2 * r, 2 * r + 1):
            absorb(tile, all_scores[tile], values2)
        attended(r, puts[r])
        for n in sent[r]:
            copies[n].start()
        for tile in range(LOOK + 2 * r, min(LOOK + 2 * r + 2, TILES)):
            all_scores.append(logits(tile, keys2))

    def a_wait(tok, source, block, device):
        ref = abuf.at[tok, source, block]
        remote(ref, ref, a_send.at[0], a_recv.at[tok, source, block], device).wait_recv()

    def project(tok, j):
        total = None
        for source in range(2):
            rows = abuf[tok, source].reshape(2 * QT, BLK)
            term = jnp.dot(
                rows,
                wall[source * BLK : (source + 1) * BLK, pl.ds(pl.multiple_of(j * CC, CC), CC)],
                preferred_element_type=f32,
            )
            total = term if total is None else total + term
        return total

    def y_copy(j):
        return remote(p0buf.at[j], prec.at[j], y_send.at[j], y_recv.at[j], nb_dev)

    a_wait(0, 0, 1 - c, sib_dev)
    a_wait(0, 1, c, pr_dev)
    a_wait(0, 1, 1 - c, pr_cross)

    def send_part(j, carry):
        for u in range(SHARED):

            @pl.when(j == u * SHARED_COLS // CC)
            def _():
                w_across(u, 1 - x).wait_recv()

        for u in range(WHOLE):

            @pl.when(j == (SHARED * SHARED_COLS + u * WHOLE_COLS) // CC)
            def _():
                w_unit(SHARED + u).wait_recv()

        p0buf[j] = project(0, j).astype(bf16)
        y_copy(j).start()
        return carry

    w_local.wait()
    lax.fori_loop(0, NCH, send_part, 0)

    a_wait(1, 0, 1 - c, sib_dev)
    a_wait(1, 1, c, pr_dev)
    a_wait(1, 1, 1 - c, pr_cross)

    def own_part(j, carry):
        p1buf[j] = project(1, j)
        return carry

    lax.fori_loop(0, NCH, own_part, 0)

    mine = pl.multiple_of(e * 64, 64)
    other = pl.multiple_of((1 - e) * 64, 64)

    def xh_copy(block_is_own, j):
        n = 0 if block_is_own else 1
        device = e_dev if block_is_own else e_cross
        return remote(
            xsend.at[n, j], xrec.at[c, j], xh_send.at[n, j], xh_recv.at[c, j], device
        )

    def sb_copy(j):
        return remote(ssend.at[j], srec.at[j], sb_send.at[j], sb_recv.at[j], sib_dev)

    def xh_wait(source_range, j):
        ref = xrec.at[source_range, j]
        remote(ref, ref, xh_send.at[0, j], xh_recv.at[source_range, j], e_dev).wait_recv()

    def finish(j):
        xh_wait(c, j)
        cols = w_cols(j)
        kept_rows = pl.ds(pl.multiple_of(c * QT + mine, 64), 64)
        value = p1buf[j, kept_rows, :] + xrec[c, j].astype(f32)
        comb[:, cols] = (value + resbuf[:, cols].astype(f32)).astype(bf16)
        xh_wait(1 - c, j)
        sb_copy(j).wait_recv()
        cols = pl.ds(pl.multiple_of((1 - c) * HALF + j * CC, 128), CC)
        value = srec[j].astype(f32) + xrec[1 - c, j].astype(f32)
        comb[:, cols] = (value + resbuf[:, cols].astype(f32)).astype(bf16)

    def after_y(j, carry):
        y_copy(j).wait_recv()

        def summed(first):
            rows = pl.ds(pl.multiple_of(first, 64), 64)
            return p1buf[j, rows, :] + prec[j, rows, :].astype(f32)

        own_base = c * QT
        sib_base = (1 - c) * QT
        xsend[0, j] = summed(own_base + other).astype(bf16)
        xh_copy(True, j).start()
        xsend[1, j] = summed(sib_base + other).astype(bf16)
        xh_copy(False, j).start()
        ssend[j] = summed(sib_base + mine).astype(bf16)
        sb_copy(j).start()
        p1buf[j, pl.ds(pl.multiple_of(own_base + mine, 64), 64), :] = summed(own_base + mine)

        @pl.when(j >= BEHIND)
        def _():
            finish(j - BEHIND)

        return carry

    res_copy.wait()
    lax.fori_loop(0, NCH, after_y, 0)
    for j in range(NCH - BEHIND, NCH):
        finish(j)

    @pl.when(h == 0)
    def _():
        anchor(0).wait_send()
        anchor(1).wait_send()

    x_copy().wait_send()
    for direction in range(2):
        for d in range(4):
            for x_ in range(2):
                if d < 3 or x_ != direction:
                    z_copy(direction, d, z, x_).wait_send()
    for g in range(8):
        for x_ in range(2):
            s_copy(g, z, x_, x_).wait_send()
    for j in range(NCH):
        y_copy(j).wait_send()
        xh_copy(True, j).wait_send()
        xh_copy(False, j).wait_send()
        sb_copy(j).wait_send()
    for u in range(SHARED + WHOLE):
        w_unit(u).wait_send()
    for j in range(SHARED):
        w_across(j, x).wait_send()
    for copy in a_copies():
        copy.wait_send()


def norm_kernel(comb, gain, stream_ref, normed_ref, normed, sems):
    keep = pltpu.make_async_copy(comb, stream_ref, sems.at[0])
    keep.start()
    gains = gain[...].astype(f32)[None, :]
    gives = []
    for n in range(64 // PART):
        rows = pl.ds(n * PART, PART)
        value = comb[rows, :].astype(f32)
        factor = lax.rsqrt(jnp.mean(value * value, axis=1, keepdims=True) + 1e-05)
        normed[rows, :] = (value * factor * gains).astype(bf16)
        give = pltpu.make_async_copy(normed.at[rows], normed_ref.at[rows], sems.at[1 + n])
        give.start()
        gives.append(give)
    keep.wait()
    for give in gives:
        give.wait()


def on_device(queries, key_states, value_states, passing, out_weight, residual, norm_gain):
    vmem = pl.BlockSpec(memory_space=pltpu.VMEM)
    anywhere = pl.BlockSpec(memory_space=pl.ANY)
    dma = pltpu.SemaphoreType.DMA
    out = jax.ShapeDtypeStruct((64, D), bf16)
    combined = pl.pallas_call(
        kernel,
        out_shape=out,
        in_specs=[anywhere] * 6,
        out_specs=vmem,
        scratch_shapes=[
            pltpu.VMEM((8, 2, 2, 2, RET, HEAD), bf16),
            pltpu.VMEM((4, HEADS * QT, 2 * HEAD), bf16),
            pltpu.VMEM((HEADS * BLK, 2 * HEAD), f32),
            pltpu.VMEM((HEADS * BLK, HEAD), f32),
            pltpu.VMEM((2 * BLK, HALF), bf16),
            pltpu.VMEM((2, 2, 2, QT, BLK), bf16),
            pltpu.VMEM((2, QT, BLK), bf16),
            pltpu.VMEM((NCH, 2 * QT, CC), bf16),
            pltpu.VMEM((NCH, 2 * QT, CC), bf16),
            pltpu.VMEM((NCH, 2 * QT, CC), f32),
            pltpu.VMEM((2, NCH, 64, CC), bf16),
            pltpu.VMEM((2, NCH, 64, CC), bf16),
            pltpu.VMEM((NCH, 64, CC), bf16),
            pltpu.VMEM((NCH, 64, CC), bf16),
            pltpu.VMEM((64, D), bf16),
            pltpu.VMEM((BLK, HEADS * HEAD), bf16),
            pltpu.VMEM((BLK, HEAD), bf16),
            pltpu.VMEM((BLK, HEAD), bf16),
            pltpu.VMEM((1, RET), jnp.int32),
            dma((4,)),
            dma((2,)),
            dma((2,)),
            dma((1,)),
            dma((1,)),
            dma((2, 4, 2)),
            dma((2, 4, 2)),
            dma((8, 2)),
            dma((8, 2)),
            dma,
            dma((SHARED + WHOLE,)),
            dma((SHARED + WHOLE,)),
            dma((SHARED,)),
            dma((SHARED,)),
            dma((6,)),
            dma((2, 2, 2)),
            dma((NCH,)),
            dma((NCH,)),
            dma((2, NCH)),
            dma((2, NCH)),
            dma((NCH,)),
            dma((NCH,)),
            dma,
        ],
        compiler_params=pltpu.CompilerParams(
            collective_id=0, has_side_effects=True, vmem_limit_bytes=58 << 20
        ),
        name="layer",
    )(
        queries,
        key_states,
        value_states,
        passing,
        out_weight,
        residual,
    )
    return pl.pallas_call(
        norm_kernel,
        out_shape=(out, out),
        in_specs=[vmem, vmem],
        out_specs=(anywhere, anywhere),
        scratch_shapes=[pltpu.VMEM((64, D), bf16), dma((1 + 64 // PART,))],
        name="norm",
    )(combined, norm_gain)


def solution(mesh):
    placed = (
        P("hst", "tp"),
        P("hst", "tp"),
        P("hst", "tp"),
        P("hst", None),
        P("tp", None),
        P(("hst", "tp"), None),
        P(),
    )
    return jax.shard_map(
        on_device,
        mesh=mesh,
        in_specs=placed,
        out_specs=(P(("hst", "tp"), None), P(("hst", "tp"), None)),
        check_vma=False,
    )
```
